32 devices in a mesh: groups: 2 (over y), ctx: 16 (over z, x, core).
Axes of the slice: x: 2, y: 2, z: 4, core: 2. Of those that a mesh axis runs over, the one named last changes fastest.
Arguments:
- queries: bfloat16 [4096, 512], P(('groups', 'ctx')), parts along dimension 0, may hold values from -150 to 150
- keys: bfloat16 [4096, 512], P(('groups', 'ctx')), parts along dimension 0, may hold values from -6 to 6
- values: bfloat16 [4096, 512], P(('groups', 'ctx')), parts along dimension 0, may hold values from -6 to 6
- cotangent: bfloat16 [4096, 512], P(('groups', 'ctx')), parts along dimension 0, may hold values from -6 to 6
Outputs:
- attended: bfloat16 [4096, 512], P(('groups', 'ctx')), parts along dimension 0
- query_grad: bfloat16 [4096, 512], P(('groups', 'ctx')), parts along dimension 0
- key_grad: bfloat16 [4096, 512], P(('groups', 'ctx')), parts along dimension 0
- value_grad: bfloat16 [4096, 512], P(('groups', 'ctx')), parts along dimension 0
The draws below stay inside these ranges and needn't reach their ends.
There are 2 independent parts, one for each index of `groups`. The reference program is written for one: setup_inputs(seed, part) draws one part's arguments, and reference() takes and returns one part's arrays. A program takes and returns all parts, laid end to end along the dimension named above; each array names one. Nothing has to cross between parts.
All inputs are finite; a program needn't handle non-finite values.
Results may differ from the reference program's by a relative error of at most 0.022.
Values may be sent and summed in bfloat16 or wider, within the bound.
A program may use at most 64 MiB of HBM per device.

```python
import jax
import jax.numpy as jnp
from jax import lax

HEADS = 4
HEAD_DIM = 128
BLOCK = 128
TOK_DEV = 128
TOKENS = 2048
N_CTX = 16


def shared_keys(key):
    base = jax.random.normal(key, (TOKENS, HEADS * HEAD_DIM), jnp.float32)
    return jnp.clip(base, -6.0, 6.0)


def draw_keys(key, part):
    base = shared_keys(key)
    return base.astype(jnp.bfloat16)


def draw_queries(key, part):
    key = jax.random.fold_in(key, 5)
    drawn = jnp.clip(2.5 * jax.random.normal(key, (TOKENS, HEADS * HEAD_DIM), jnp.float32), -15.0, 15.0)
    return drawn.astype(jnp.bfloat16)


def steps_of(rng, dims, split, smallest, high):
    def one(position, parts):
        draws = jax.random.uniform(jax.random.fold_in(jax.random.fold_in(rng, 6), position), (parts,), jnp.float32, smallest / len(split), high / len(split))
        return jnp.repeat(jnp.exp(draws), dims[position] // parts).reshape((-1,) + (1,) * (len(dims) - position - 1))

    factor_of = one(*split[0])
    for cut in split[1:]:
        factor_of = factor_of * one(*cut)
    return factor_of


def gaussian(own_key, extent, deviation, reach, split=(), kind=jnp.bfloat16):
    array = deviation * jax.random.normal(own_key, extent, jnp.float32)
    if split:
        array = array * steps_of(own_key, extent, split, -0.22, 0.18)
    return jnp.clip(array, -reach, reach).astype(kind)


def setup_inputs(seed: int = 0, part: int = 0) -> dict:
    key_of = jax.random.split(jax.random.key(seed), 5)
    part_splits = jax.random.split(jax.random.fold_in(key_of[4], part), 5)
    queries = draw_queries(jax.random.fold_in(jax.random.fold_in(key_of[4], part), 71), part)
    keys = draw_keys(jax.random.fold_in(jax.random.fold_in(key_of[4], part), 71), part)
    values = gaussian(part_splits[2], (TOKENS, HEADS * HEAD_DIM), 1.0, 6.0, ((0, 16),))
    cotangent = gaussian(part_splits[3], (TOKENS, HEADS * HEAD_DIM), 1.0, 6.0, ((0, 16),))
    return dict(queries=queries, keys=keys, values=values, cotangent=cotangent)


ROOT_HALF = 0.70710678


def pool_rows(pairs):
    widened = pairs.astype(jnp.float32).reshape(pairs.shape[0] // 2, 2, pairs.shape[1])
    return ((widened[:, 0] + widened[:, 1]) * ROOT_HALF).astype(jnp.bfloat16)


def swap_halves(blocks):
    count_now = blocks.shape[0]
    folded = blocks.reshape((count_now // 2, 2) + blocks.shape[1:])
    return jnp.flip(folded, axis=1).reshape(blocks.shape)


def attend_sets(queries, cotangent, pair_sets, groups):
    row_count = queries.shape[0]
    model_cols = queries.shape[1]
    set_width = pair_sets[0].shape[1]
    score_scale = HEAD_DIM ** -0.5
    attended_heads = []
    query_heads = []
    key_heads = [[] for member in pair_sets]
    value_heads = [[] for member in pair_sets]
    for head_index in range(HEADS):
        low_col = head_index * HEAD_DIM
        q_head = queries[:, low_col:low_col + HEAD_DIM].astype(jnp.float32)
        d_head = cotangent[:, low_col:low_col + HEAD_DIM].astype(jnp.float32)
        key_parts = []
        value_parts = []
        score_list = []
        for pair_set, group_size in zip(pair_sets, groups):
            key_part = pair_set[:, :, low_col:low_col + HEAD_DIM].astype(jnp.float32)
            value_part = pair_set[:, :, model_cols + low_col:model_cols + low_col + HEAD_DIM].astype(jnp.float32)
            key_parts.append(key_part)
            value_parts.append(value_part)
            q_group = q_head.reshape(row_count // group_size, group_size, HEAD_DIM)
            score_list.append(jnp.einsum("gsd,gkd->gsk", q_group, key_part).reshape(row_count, set_width))
        scores = jnp.stack(score_list, axis=0) * score_scale
        peak = jnp.max(scores, axis=(0, 2))
        weights = jnp.exp(scores - peak[None, :, None])
        probs = weights / jnp.sum(weights, axis=(0, 2))[None, :, None]
        probs_low = probs.astype(jnp.bfloat16).astype(jnp.float32)
        output = jnp.zeros((row_count, HEAD_DIM), jnp.float32)
        dprob_list = []
        for set_index in range(len(pair_sets)):
            group_size = groups[set_index]
            p_group = probs_low[set_index].reshape(row_count // group_size, group_size, set_width)
            output = output + jnp.einsum("gsk,gkd->gsd", p_group, value_parts[set_index]).reshape(row_count, HEAD_DIM)
            d_group = d_head.reshape(row_count // group_size, group_size, HEAD_DIM)
            dprob_list.append(jnp.einsum("gsd,gkd->gsk", d_group, value_parts[set_index]).reshape(row_count, set_width))
        attended = output.astype(jnp.bfloat16)
        delta = jnp.sum(d_head * attended.astype(jnp.float32), axis=1)
        dprobs = jnp.stack(dprob_list, axis=0)
        dscores = (score_scale * probs * (dprobs - delta[None, :, None])).astype(jnp.bfloat16).astype(jnp.float32)
        query_total = jnp.zeros((row_count, HEAD_DIM), jnp.float32)
        for set_index in range(len(pair_sets)):
            group_size = groups[set_index]
            s_group = dscores[set_index].reshape(row_count // group_size, group_size, set_width)
            p_group = probs_low[set_index].reshape(row_count // group_size, group_size, set_width)
            q_group = q_head.reshape(row_count // group_size, group_size, HEAD_DIM)
            d_group = d_head.reshape(row_count // group_size, group_size, HEAD_DIM)
            query_total = query_total + jnp.einsum("gsk,gkd->gsd", s_group, key_parts[set_index]).reshape(row_count, HEAD_DIM)
            key_heads[set_index].append(jnp.einsum("gsk,gsd->gkd", s_group, q_group))
            value_heads[set_index].append(jnp.einsum("gsk,gsd->gkd", p_group, d_group))
        attended_heads.append(attended)
        query_heads.append(query_total)
    set_grads = [jnp.concatenate(key_heads[set_index] + value_heads[set_index], axis=2) for set_index in range(len(pair_sets))]
    return jnp.concatenate(attended_heads, axis=1), jnp.concatenate(query_heads, axis=1), set_grads


def reference(queries, keys, values, cotangent):
    token_total, model_cols = queries.shape
    block_count = TOK_DEV // BLOCK
    local_levels = block_count.bit_length() - 1
    all_levels = (token_total // BLOCK).bit_length() - 1
    pair_level = [jnp.concatenate([keys, values], axis=1)]
    for level_index in range(1, all_levels):
        pair_level.append(pool_rows(pair_level[-1]))
    far_init = tuple(jnp.zeros((token_total >> level_index, 2 * model_cols), jnp.float32) for level_index in range(local_levels, all_levels))

    def visit(carried, device):
        q_block = lax.dynamic_slice_in_dim(queries, device * TOK_DEV, TOK_DEV, 0)
        d_block = lax.dynamic_slice_in_dim(cotangent, device * TOK_DEV, TOK_DEV, 0)
        own_pairs = lax.dynamic_slice_in_dim(pair_level[0], device * TOK_DEV, TOK_DEV, 0)
        pair_sets = [own_pairs.reshape(block_count, BLOCK, 2 * model_cols)]
        groups = [BLOCK]
        for level_index in range(local_levels):
            level_rows = TOK_DEV >> level_index
            local_pairs = lax.dynamic_slice_in_dim(pair_level[level_index], device * level_rows, level_rows, 0)
            pair_sets.append(swap_halves(local_pairs.reshape(level_rows // BLOCK, BLOCK, 2 * model_cols)))
            groups.append(BLOCK << level_index)
        starts = []
        for level_index in range(local_levels, all_levels):
            span_devices = 1 << (level_index - local_levels)
            partner = jnp.bitwise_xor(device // span_devices, 1) * BLOCK
            starts.append(partner)
            far_pairs = lax.dynamic_slice_in_dim(pair_level[level_index], partner, BLOCK, 0)
            pair_sets.append(far_pairs.reshape(1, BLOCK, 2 * model_cols))
            groups.append(TOK_DEV)
        attended, query_grad, set_grads = attend_sets(q_block, d_block, pair_sets, groups)
        updated = []
        for place in range(all_levels - local_levels):
            store = carried[place]
            current = lax.dynamic_slice_in_dim(store, starts[place], BLOCK, 0)
            fresh = current + set_grads[1 + local_levels + place].reshape(BLOCK, 2 * model_cols)
            updated.append(lax.dynamic_update_slice_in_dim(store, fresh, starts[place], 0))
        local_out = [set_grads[0].reshape(TOK_DEV, 2 * model_cols)]
        for level_index in range(local_levels):
            local_out.append(swap_halves(set_grads[1 + level_index]).reshape(TOK_DEV >> level_index, 2 * model_cols))
        return tuple(updated), (attended, query_grad.astype(jnp.bfloat16), tuple(local_out))

    far_grads, outputs = lax.scan(visit, far_init, jnp.arange(N_CTX, dtype=jnp.int32))
    attended, query_grad, local_out = outputs
    grads = []
    for level_index in range(all_levels):
        if level_index < local_levels:
            grads.append(local_out[1 + level_index].reshape(token_total >> level_index, 2 * model_cols))
        else:
            grads.append(far_grads[level_index - local_levels])
    grads[0] = grads[0] + local_out[0].reshape(token_total, 2 * model_cols)
    for level_index in range(all_levels - 1, 0, -1):
        grads[level_index - 1] = grads[level_index - 1] + jnp.repeat(grads[level_index], 2, axis=0) * ROOT_HALF
    attended = attended.reshape(token_total, model_cols)
    query_grad = query_grad.reshape(token_total, model_cols)
    key_grad = grads[0][:, :model_cols].astype(jnp.bfloat16)
    value_grad = grads[0][:, model_cols:].astype(jnp.bfloat16)
    return attended, query_grad, key_grad, value_grad
```

```python
import functools

import jax
import jax.numpy as jnp
from jax import lax
from jax.experimental import pallas as pl
from jax.experimental.pallas import tpu as pltpu
from jax.sharding import PartitionSpec as P

HEADS = 4
HEAD_DIM = 128
BLOCK = 128


ROOT_HALF = 0.70710678


def swapped(value, axis, stride):
    mask = 2**stride
    pairs = [(source, source ^ mask) for source in range(lax.axis_size(axis))]
    return lax.ppermute(value, axis, pairs)


def pool_rows(pairs):
    widened = pairs.astype(jnp.float32).reshape(pairs.shape[0] // 2, 2, pairs.shape[1])
    return ((widened[:, 0] + widened[:, 1]) * ROOT_HALF).astype(jnp.bfloat16)


def attend_sets(queries, cotangent, pair_sets, groups):
    row_count = queries.shape[0]
    model_cols = queries.shape[1]
    set_width = pair_sets[0].shape[1]
    score_scale = HEAD_DIM ** (-0.5)
    attended_heads = []
    query_heads = []
    key_heads = [[] for member in pair_sets]
    value_heads = [[] for member in pair_sets]
    for head_index in range(HEADS):
        low_col = head_index * HEAD_DIM
        q_head = queries[:, low_col : low_col + HEAD_DIM]
        d_head = cotangent[:, low_col : low_col + HEAD_DIM]
        key_parts = []
        value_parts = []
        score_list = []
        for pair_set, group_size in zip(pair_sets, groups):
            key_part = pair_set[:, :, low_col : low_col + HEAD_DIM]
            value_part = pair_set[:, :, model_cols + low_col : model_cols + low_col + HEAD_DIM]
            key_parts.append(key_part)
            value_parts.append(value_part)
            q_group = q_head.reshape(row_count // group_size, group_size, HEAD_DIM)
            score_list.append(
                jnp.einsum(
                    "gsd,gkd->gsk", q_group, key_part, preferred_element_type=jnp.float32
                ).reshape(row_count, set_width)
            )
        scores = jnp.stack(score_list, axis=0) * score_scale
        peak = jnp.max(scores, axis=(0, 2))
        weights = jnp.exp(scores - peak[None, :, None])
        probs = weights / jnp.sum(weights, axis=(0, 2))[None, :, None]
        probs_low = probs.astype(jnp.bfloat16)
        output = jnp.zeros((row_count, HEAD_DIM), jnp.float32)
        dprob_list = []
        for set_index in range(len(pair_sets)):
            group_size = groups[set_index]
            p_group = probs_low[set_index].reshape(row_count // group_size, group_size, set_width)
            output = output + jnp.einsum(
                "gsk,gkd->gsd", p_group, value_parts[set_index], preferred_element_type=jnp.float32
            ).reshape(row_count, HEAD_DIM)
            d_group = d_head.reshape(row_count // group_size, group_size, HEAD_DIM)
            dprob_list.append(
                jnp.einsum(
                    "gsd,gkd->gsk",
                    d_group,
                    value_parts[set_index],
                    preferred_element_type=jnp.float32,
                ).reshape(row_count, set_width)
            )
        attended = output.astype(jnp.bfloat16)
        delta = jnp.sum(d_head.astype(jnp.float32) * attended.astype(jnp.float32), axis=1)
        dprobs = jnp.stack(dprob_list, axis=0)
        dscores = (score_scale * probs * (dprobs - delta[None, :, None])).astype(jnp.bfloat16)
        query_total = jnp.zeros((row_count, HEAD_DIM), jnp.float32)
        for set_index in range(len(pair_sets)):
            group_size = groups[set_index]
            s_group = dscores[set_index].reshape(row_count // group_size, group_size, set_width)
            p_group = probs_low[set_index].reshape(row_count // group_size, group_size, set_width)
            q_group = q_head.reshape(row_count // group_size, group_size, HEAD_DIM)
            d_group = d_head.reshape(row_count // group_size, group_size, HEAD_DIM)
            query_total = query_total + jnp.einsum(
                "gsk,gkd->gsd", s_group, key_parts[set_index], preferred_element_type=jnp.float32
            ).reshape(row_count, HEAD_DIM)
            key_heads[set_index].append(
                jnp.einsum("gsk,gsd->gkd", s_group, q_group, preferred_element_type=jnp.float32)
            )
            value_heads[set_index].append(
                jnp.einsum("gsk,gsd->gkd", p_group, d_group, preferred_element_type=jnp.float32)
            )
        attended_heads.append(attended)
        query_heads.append(query_total)
    set_grads = [
        jnp.concatenate(key_heads[set_index] + value_heads[set_index], axis=2)
        for set_index in range(len(pair_sets))
    ]
    return (
        jnp.concatenate(attended_heads, axis=1),
        jnp.concatenate(query_heads, axis=1),
        set_grads,
    )


def upper_member(position, bit_number):
    return position // (1 << bit_number) % 2 == 1


def per_device_chained(queries, keys, values, cotangent):
    tok_count, model_cols = queries.shape
    ctx_count = lax.axis_size("ctx")
    position = lax.axis_index("ctx")
    block_count = tok_count // BLOCK
    local_levels = block_count.bit_length() - 1
    all_levels = (block_count * ctx_count).bit_length() - 1
    pair_level = [jnp.concatenate([keys, values], axis=1)]
    for level_index in range(1, all_levels):
        pair_level.append(pool_rows(pair_level[-1]))
    pair_sets = [pair_level[0].reshape(block_count, BLOCK, 2 * model_cols)]
    groups = [BLOCK]
    far_pairs = [None for level_index in range(local_levels, all_levels)]
    own_pairs = pair_level[local_levels]
    for level_index in range(local_levels, all_levels):
        bit_number = level_index - local_levels
        received = swapped(own_pairs, "ctx", bit_number)
        far_pairs[bit_number] = received
        if level_index + 1 < all_levels:
            upper = upper_member(position, bit_number)
            joined = jnp.where(
                upper,
                jnp.concatenate([received, own_pairs], axis=0),
                jnp.concatenate([own_pairs, received], axis=0),
            )
            own_pairs = pool_rows(joined)
    for level_index in range(local_levels, all_levels):
        pair_sets.append(far_pairs[level_index - local_levels].reshape(1, BLOCK, 2 * model_cols))
        groups.append(tok_count)
    attended, query_grad, set_grads = attend_sets(queries, cotangent, pair_sets, groups)
    grads = [
        jnp.zeros((tok_count >> level_index, 2 * model_cols), jnp.float32)
        for level_index in range(all_levels)
    ]
    grads[0] = set_grads[0].reshape(tok_count, 2 * model_cols)
    far_grads = [
        set_grads[1 + level_index].reshape(BLOCK, 2 * model_cols)
        for level_index in range(local_levels, all_levels)
    ]
    carried = None
    for level_index in reversed(range(local_levels, all_levels)):
        bit_number = level_index - local_levels
        outgoing = far_grads[bit_number]
        if carried is None:
            kept = jnp.zeros((BLOCK, 2 * model_cols), jnp.float32)
        else:
            spread = jnp.repeat(carried, 2, axis=0) * ROOT_HALF
            lower_half = spread[:BLOCK]
            upper_half = spread[BLOCK:]
            upper = upper_member(position, bit_number)
            kept = jnp.where(upper, upper_half, lower_half)
            outgoing = outgoing + jnp.where(upper, lower_half, upper_half)
        carried = kept + swapped(outgoing, "ctx", bit_number)
    grads[local_levels] = grads[local_levels] + carried
    for level_index in range(all_levels - 1, 0, -1):
        grads[level_index - 1] = (
            grads[level_index - 1] + jnp.repeat(grads[level_index], 2, axis=0) * ROOT_HALF
        )
    key_grad = grads[0][:, :model_cols].astype(jnp.bfloat16)
    value_grad = grads[0][:, model_cols:].astype(jnp.bfloat16)
    return (attended, query_grad.astype(jnp.bfloat16), key_grad, value_grad)


def chunk_slot(level, member):
    return (1 << level) - 2 + member


def contract(left, right, left_dim, right_dim):
    return lax.dot_general(
        left, right, (((left_dim,), (right_dim,)), ((), ())), preferred_element_type=jnp.float32
    )


def exchange_kernel(
    levels,
    q_ref,
    k_ref,
    v_ref,
    d_ref,
    att_ref,
    dq_ref,
    dk_ref,
    dv_ref,
    wide,
    pooled,
    q_all,
    d_all,
    kv_all,
    grad_out,
    grad_in,
    near_out,
    near_in,
    att_out,
    dq_out,
    spread,
    pool_send,
    pool_recv,
    near_send,
    near_recv,
    grad_send,
    grad_recv,
    back_send,
    back_recv,
):
    me = lax.axis_index("ctx")
    count = 1 << levels
    core = lax.rem(me, 2)
    sibling = me + 1 - 2 * core
    half = 2 * HEAD_DIM
    own_cols = pl.ds(pl.multiple_of(core * half, half), half)
    sib_cols = pl.ds(pl.multiple_of(half - core * half, half), half)

    def remote(src, dst, send, recv, target):
        return pltpu.make_async_remote_copy(
            src_ref=src,
            dst_ref=dst,
            send_sem=send,
            recv_sem=recv,
            device_id={"ctx": target},
            device_id_type=pl.DeviceIdType.MESH,
        )

    barrier = pltpu.get_barrier_semaphore()
    for step in range(1, count):
        other = lax.rem(me + step, count)
        pl.semaphore_signal(
            barrier, inc=1, device_id={"ctx": other}, device_id_type=pl.DeviceIdType.MESH
        )

    for c in range(2):
        for part in range(4):
            src = k_ref if part < 2 else v_ref
            low_col = c * half + part % 2 * HEAD_DIM
            wide[c * 4 + part] = src[:, low_col : low_col + HEAD_DIM].astype(jnp.float32)
    for level in range(1, levels):
        rows = BLOCK >> level
        base = BLOCK - 2 * rows
        for c in range(2):
            for part in range(4):
                column = wide.at[c * 4 + part]
                even = column[pl.ds(0, rows, stride=2), :]
                odd = column[pl.ds(1, rows, stride=2), :]
                low = ((even + odd) * ROOT_HALF).astype(jnp.bfloat16)
                pooled[c, base : base + rows, part * HEAD_DIM : (part + 1) * HEAD_DIM] = low
                if level + 1 < levels:
                    column[0:rows, :] = low.astype(jnp.float32)
    pl.semaphore_wait(barrier, count - 1)

    def pool_copy(level, member):
        rows = BLOCK >> level
        base = BLOCK - 2 * rows
        size = 1 << level
        mine = lax.rem(me, size)
        group = lax.div(me, size)
        partner = group + 1 - 2 * lax.rem(group, 2)
        return remote(
            pooled.at[member % 2, pl.ds(base, rows), :],
            kv_all.at[pl.ds(pl.multiple_of(BLOCK * (level + 1) + mine * rows, rows), rows), :],
            pool_send.at[chunk_slot(level, member)],
            pool_recv.at[chunk_slot(level, 0) + mine],
            partner * size + member,
        )

    def pool_arrival(level, member):
        rows = BLOCK >> level
        base = BLOCK - 2 * rows
        return remote(
            pooled.at[0, pl.ds(base, rows), :],
            kv_all.at[pl.ds(BLOCK * (level + 1) + member * rows, rows), :],
            pool_send.at[chunk_slot(level, member)],
            pool_recv.at[chunk_slot(level, member)],
            sibling,
        )

    own_rows = pl.ds(pl.multiple_of(core * BLOCK, BLOCK), BLOCK)
    sib_rows = pl.ds(pl.multiple_of(BLOCK - core * BLOCK, BLOCK), BLOCK)
    near = [
        remote(src.at[:, sib_cols], dst, near_send.at[i], near_recv.at[i], sibling)
        for i, (src, dst) in enumerate(
            [
                (q_ref, q_all.at[own_rows, :]),
                (k_ref, kv_all.at[own_rows, pl.ds(0, half)]),
                (v_ref, kv_all.at[own_rows, pl.ds(half, half)]),
                (d_ref, d_all.at[own_rows, :]),
            ]
        )
    ]
    pool_copies = [
        pool_copy(level, member) for level in reversed(range(1, levels)) for member in range(1 << level)
    ]
    for copy in near:
        copy.start()
    for copy in pool_copies:
        copy.start()
    q_all[own_rows, :] = q_ref[:, own_cols]
    d_all[own_rows, :] = d_ref[:, own_cols]
    kv_all[own_rows, 0:half] = k_ref[:, own_cols]
    kv_all[own_rows, half : 2 * half] = v_ref[:, own_cols]
    for copy in near:
        copy.wait_recv()

    segments = [(0, 2 * BLOCK)] + [(BLOCK * (level + 1), BLOCK) for level in range(1, levels)]
    score_scale = HEAD_DIM ** (-0.5)
    scores = [[], []]
    dprobs = [[], []]
    q_heads = [q_all[:, h * HEAD_DIM : (h + 1) * HEAD_DIM] for h in range(2)]
    d_heads = [d_all[:, h * HEAD_DIM : (h + 1) * HEAD_DIM] for h in range(2)]

    def k_part(index, h):
        low, rows = segments[index]
        return kv_all[low : low + rows, h * HEAD_DIM : (h + 1) * HEAD_DIM]

    def v_part(index, h):
        low, rows = segments[index]
        return kv_all[low : low + rows, half + h * HEAD_DIM : half + (h + 1) * HEAD_DIM]

    for index in range(levels):
        if index > 0:
            for member in range(1 << index):
                pool_arrival(index, member).wait_recv()
        for h in range(2):
            scores[h].append(contract(q_heads[h], k_part(index, h), 1, 1) * score_scale)
            dprobs[h].append(contract(d_heads[h], v_part(index, h), 1, 1))

    def grad_copy(level, member):
        rows = BLOCK >> level
        size = 1 << level
        mine = lax.rem(me, size)
        group = lax.div(me, size)
        partner = group + 1 - 2 * lax.rem(group, 2)
        return remote(
            grad_out.at[level - 1, pl.ds(member * rows, rows), :],
            grad_in.at[level - 1, pl.ds(pl.multiple_of(mine * rows, rows), rows), :],
            grad_send.at[chunk_slot(level, member)],
            grad_recv.at[chunk_slot(level, 0) + mine],
            partner * size + member,
        )

    def grad_arrival(level, member):
        rows = BLOCK >> level
        return remote(
            grad_out.at[level - 1, pl.ds(member * rows, rows), :],
            grad_in.at[level - 1, pl.ds(member * rows, rows), :],
            grad_send.at[chunk_slot(level, member)],
            grad_recv.at[chunk_slot(level, member)],
            sibling,
        )

    near_grads = []
    for h in range(2):
        low_col = h * HEAD_DIM
        peak = jnp.max(scores[h][0], axis=1, keepdims=True)
        for part in scores[h][1:]:
            peak = jnp.maximum(peak, jnp.max(part, axis=1, keepdims=True))
        weights = [jnp.exp(part - peak) for part in scores[h]]
        total = jnp.sum(weights[0], axis=1, keepdims=True)
        for part in weights[1:]:
            total = total + jnp.sum(part, axis=1, keepdims=True)
        inverse = 1.0 / total
        probs = [part * inverse for part in weights]
        probs_low = [part.astype(jnp.bfloat16) for part in probs]
        output = contract(probs_low[0], v_part(0, h), 1, 0)
        for index in range(1, levels):
            output = output + contract(probs_low[index], v_part(index, h), 1, 0)
        attended = output.astype(jnp.bfloat16)
        att_out[:, low_col : low_col + HEAD_DIM] = attended
        delta = jnp.sum(
            d_heads[h].astype(jnp.float32) * attended.astype(jnp.float32), axis=1, keepdims=True
        )
        dscores = [
            (score_scale * part * (dpart - delta)).astype(jnp.bfloat16)
            for part, dpart in zip(probs, dprobs[h])
        ]
        for index in range(1, levels):
            grad_out[index - 1, :, low_col : low_col + HEAD_DIM] = contract(
                dscores[index], q_heads[h], 0, 0
            ).astype(jnp.bfloat16)
            grad_out[index - 1, :, half + low_col : half + low_col + HEAD_DIM] = contract(
                probs_low[index], d_heads[h], 0, 0
            ).astype(jnp.bfloat16)
        near_grads.append((dscores, probs_low))
    grad_copies = [
        grad_copy(level, member) for level in reversed(range(1, levels)) for member in range(1 << level)
    ]
    for copy in grad_copies:
        copy.start()
    for h in range(2):
        low_col = h * HEAD_DIM
        dscores, probs_low = near_grads[h]
        near_out[:, low_col : low_col + HEAD_DIM] = contract(dscores[0], q_heads[h], 0, 0).astype(jnp.bfloat16)
        near_out[:, half + low_col : half + low_col + HEAD_DIM] = contract(
            probs_low[0], d_heads[h], 0, 0
        ).astype(jnp.bfloat16)
        query_total = contract(dscores[0], k_part(0, h), 1, 0)
        for index in range(1, levels):
            query_total = query_total + contract(dscores[index], k_part(index, h), 1, 0)
        dq_out[:, low_col : low_col + HEAD_DIM] = query_total.astype(jnp.bfloat16)
    back = [
        remote(near_out.at[sib_rows, :], near_in.at[core], back_send.at[0], back_recv.at[0], sibling),
        remote(att_out.at[sib_rows, :], att_ref.at[:, own_cols], back_send.at[1], back_recv.at[1], sibling),
        remote(dq_out.at[sib_rows, :], dq_ref.at[:, own_cols], back_send.at[2], back_recv.at[2], sibling),
    ]
    for copy in back:
        copy.start()
    near_in[core] = near_out[own_rows, :]
    att_ref[:, own_cols] = att_out[own_rows, :]
    dq_ref[:, own_cols] = dq_out[own_rows, :]
    for level in reversed(range(1, levels)):
        for member in range(1 << level):
            grad_arrival(level, member).wait_recv()
    back[0].wait_recv()
    for c in range(2):
        carried = None
        for level in reversed(range(1, levels)):
            rows = BLOCK >> level
            for member in range(c, 1 << level, 2):
                part = grad_in[level - 1, member * rows : (member + 1) * rows, :].astype(jnp.float32)
                carried = part if carried is None else carried + part
            carried = carried * ROOT_HALF
            for part in range(4):
                column = spread.at[part]
                piece = carried[:, part * HEAD_DIM : (part + 1) * HEAD_DIM]
                column[pl.ds(0, rows, stride=2), :] = piece
                column[pl.ds(1, rows, stride=2), :] = piece
            carried = jnp.concatenate([spread[part, 0 : 2 * rows, :] for part in range(4)], axis=1)
        carried = carried + near_in[c].astype(jnp.float32)
        low = carried.astype(jnp.bfloat16)
        dk_ref[:, c * half : (c + 1) * half] = low[:, :half]
        dv_ref[:, c * half : (c + 1) * half] = low[:, half:]
    for copy in back[1:]:
        copy.wait_recv()
    for copy in near + pool_copies + grad_copies + back:
        copy.wait_send()


def per_device(queries, keys, values, cotangent):
    tok_count, model_cols = queries.shape
    levels = lax.axis_size("ctx").bit_length() - 1
    if tok_count != BLOCK or levels < 2 or BLOCK >> (levels - 1) < 16:
        return per_device_chained(queries, keys, values, cotangent)
    chunks = (1 << levels) - 2
    half = model_cols // 2
    flat = jax.ShapeDtypeStruct((tok_count, model_cols), jnp.bfloat16)
    vmem = pl.BlockSpec(memory_space=pltpu.VMEM)
    return pl.pallas_call(
        functools.partial(exchange_kernel, levels),
        out_shape=(flat, flat, flat, flat),
        in_specs=[vmem] * 4,
        out_specs=(vmem,) * 4,
        scratch_shapes=[
            pltpu.VMEM((8, BLOCK, HEAD_DIM), jnp.float32),
            pltpu.VMEM((2, BLOCK, model_cols), jnp.bfloat16),
            pltpu.VMEM((2 * BLOCK, half), jnp.bfloat16),
            pltpu.VMEM((2 * BLOCK, half), jnp.bfloat16),
            pltpu.VMEM((BLOCK * (levels + 1), model_cols), jnp.bfloat16),
            pltpu.VMEM((levels - 1, BLOCK, model_cols), jnp.bfloat16),
            pltpu.VMEM((levels - 1, BLOCK, model_cols), jnp.bfloat16),
            pltpu.VMEM((2 * BLOCK, model_cols), jnp.bfloat16),
            pltpu.VMEM((2, BLOCK, model_cols), jnp.bfloat16),
            pltpu.VMEM((2 * BLOCK, half), jnp.bfloat16),
            pltpu.VMEM((2 * BLOCK, half), jnp.bfloat16),
            pltpu.VMEM((4, BLOCK, HEAD_DIM), jnp.float32),
            pltpu.SemaphoreType.DMA((chunks,)),
            pltpu.SemaphoreType.DMA((chunks,)),
            pltpu.SemaphoreType.DMA((4,)),
            pltpu.SemaphoreType.DMA((4,)),
            pltpu.SemaphoreType.DMA((chunks,)),
            pltpu.SemaphoreType.DMA((chunks,)),
            pltpu.SemaphoreType.DMA((3,)),
            pltpu.SemaphoreType.DMA((3,)),
        ],
        compiler_params=pltpu.CompilerParams(
            collective_id=0, has_side_effects=True, vmem_limit_bytes=32 * 1024 * 1024
        ),
    )(queries, keys, values, cotangent)


def solution(mesh):
    placed = (
        P(("groups", "ctx"), None),
        P(("groups", "ctx"), None),
        P(("groups", "ctx"), None),
        P(("groups", "ctx"), None),
    )
    return jax.shard_map(
        per_device,
        mesh=mesh,
        in_specs=placed,
        out_specs=(
            P(("groups", "ctx"), None),
            P(("groups", "ctx"), None),
            P(("groups", "ctx"), None),
            P(("groups", "ctx"), None),
        ),
        check_vma=False,
    )
```

```python
import functools

import jax
import jax.numpy as jnp
from jax import lax
from jax.experimental import pallas as pl
from jax.experimental.pallas import tpu as pltpu
from jax.sharding import PartitionSpec as P

HEADS = 4
HEAD_DIM = 128
BLOCK = 128


ROOT_HALF = 0.70710678


def swapped(value, axis, stride):
    mask = 2**stride
    pairs = [(source, source ^ mask) for source in range(lax.axis_size(axis))]
    return lax.ppermute(value, axis, pairs)


def pool_rows(pairs):
    widened = pairs.astype(jnp.float32).reshape(pairs.shape[0] // 2, 2, pairs.shape[1])
    return ((widened[:, 0] + widened[:, 1]) * ROOT_HALF).astype(jnp.bfloat16)


def attend_sets(queries, cotangent, pair_sets, groups):
    row_count = queries.shape[0]
    model_cols = queries.shape[1]
    set_width = pair_sets[0].shape[1]
    score_scale = HEAD_DIM ** (-0.5)
    attended_heads = []
    query_heads = []
    key_heads = [[] for member in pair_sets]
    value_heads = [[] for member in pair_sets]
    for head_index in range(HEADS):
        low_col = head_index * HEAD_DIM
        q_head = queries[:, low_col : low_col + HEAD_DIM]
        d_head = cotangent[:, low_col : low_col + HEAD_DIM]
        key_parts = []
        value_parts = []
        score_list = []
        for pair_set, group_size in zip(pair_sets, groups):
            key_part = pair_set[:, :, low_col : low_col + HEAD_DIM]
            value_part = pair_set[:, :, model_cols + low_col : model_cols + low_col + HEAD_DIM]
            key_parts.append(key_part)
            value_parts.append(value_part)
            q_group = q_head.reshape(row_count // group_size, group_size, HEAD_DIM)
            score_list.append(
                jnp.einsum(
                    "gsd,gkd->gsk", q_group, key_part, preferred_element_type=jnp.float32
                ).reshape(row_count, set_width)
            )
        scores = jnp.stack(score_list, axis=0) * score_scale
        peak = jnp.max(scores, axis=(0, 2))
        weights = jnp.exp(scores - peak[None, :, None])
        probs = weights / jnp.sum(weights, axis=(0, 2))[None, :, None]
        probs_low = probs.astype(jnp.bfloat16)
        output = jnp.zeros((row_count, HEAD_DIM), jnp.float32)
        dprob_list = []
        for set_index in range(len(pair_sets)):
            group_size = groups[set_index]
            p_group = probs_low[set_index].reshape(row_count // group_size, group_size, set_width)
            output = output + jnp.einsum(
                "gsk,gkd->gsd", p_group, value_parts[set_index], preferred_element_type=jnp.float32
            ).reshape(row_count, HEAD_DIM)
            d_group = d_head.reshape(row_count // group_size, group_size, HEAD_DIM)
            dprob_list.append(
                jnp.einsum(
                    "gsd,gkd->gsk",
                    d_group,
                    value_parts[set_index],
                    preferred_element_type=jnp.float32,
                ).reshape(row_count, set_width)
            )
        attended = output.astype(jnp.bfloat16)
        delta = jnp.sum(d_head.astype(jnp.float32) * attended.astype(jnp.float32), axis=1)
        dprobs = jnp.stack(dprob_list, axis=0)
        dscores = (score_scale * probs * (dprobs - delta[None, :, None])).astype(jnp.bfloat16)
        query_total = jnp.zeros((row_count, HEAD_DIM), jnp.float32)
        for set_index in range(len(pair_sets)):
            group_size = groups[set_index]
            s_group = dscores[set_index].reshape(row_count // group_size, group_size, set_width)
            p_group = probs_low[set_index].reshape(row_count // group_size, group_size, set_width)
            q_group = q_head.reshape(row_count // group_size, group_size, HEAD_DIM)
            d_group = d_head.reshape(row_count // group_size, group_size, HEAD_DIM)
            query_total = query_total + jnp.einsum(
                "gsk,gkd->gsd", s_group, key_parts[set_index], preferred_element_type=jnp.float32
            ).reshape(row_count, HEAD_DIM)
            key_heads[set_index].append(
                jnp.einsum("gsk,gsd->gkd", s_group, q_group, preferred_element_type=jnp.float32)
            )
            value_heads[set_index].append(
                jnp.einsum("gsk,gsd->gkd", p_group, d_group, preferred_element_type=jnp.float32)
            )
        attended_heads.append(attended)
        query_heads.append(query_total)
    set_grads = [
        jnp.concatenate(key_heads[set_index] + value_heads[set_index], axis=2)
        for set_index in range(len(pair_sets))
    ]
    return (
        jnp.concatenate(attended_heads, axis=1),
        jnp.concatenate(query_heads, axis=1),
        set_grads,
    )


def upper_member(position, bit_number):
    return position // (1 << bit_number) % 2 == 1


def per_device_chained(queries, keys, values, cotangent):
    tok_count, model_cols = queries.shape
    ctx_count = lax.axis_size("ctx")
    position = lax.axis_index("ctx")
    block_count = tok_count // BLOCK
    local_levels = block_count.bit_length() - 1
    all_levels = (block_count * ctx_count).bit_length() - 1
    pair_level = [jnp.concatenate([keys, values], axis=1)]
    for level_index in range(1, all_levels):
        pair_level.append(pool_rows(pair_level[-1]))
    pair_sets = [pair_level[0].reshape(block_count, BLOCK, 2 * model_cols)]
    groups = [BLOCK]
    far_pairs = [None for level_index in range(local_levels, all_levels)]
    own_pairs = pair_level[local_levels]
    for level_index in range(local_levels, all_levels):
        bit_number = level_index - local_levels
        received = swapped(own_pairs, "ctx", bit_number)
        far_pairs[bit_number] = received
        if level_index + 1 < all_levels:
            upper = upper_member(position, bit_number)
            joined = jnp.where(
                upper,
                jnp.concatenate([received, own_pairs], axis=0),
                jnp.concatenate([own_pairs, received], axis=0),
            )
            own_pairs = pool_rows(joined)
    for level_index in range(local_levels, all_levels):
        pair_sets.append(far_pairs[level_index - local_levels].reshape(1, BLOCK, 2 * model_cols))
        groups.append(tok_count)
    attended, query_grad, set_grads = attend_sets(queries, cotangent, pair_sets, groups)
    grads = [
        jnp.zeros((tok_count >> level_index, 2 * model_cols), jnp.float32)
        for level_index in range(all_levels)
    ]
    grads[0] = set_grads[0].reshape(tok_count, 2 * model_cols)
    far_grads = [
        set_grads[1 + level_index].reshape(BLOCK, 2 * model_cols)
        for level_index in range(local_levels, all_levels)
    ]
    carried = None
    for level_index in reversed(range(local_levels, all_levels)):
        bit_number = level_index - local_levels
        outgoing = far_grads[bit_number]
        if carried is None:
            kept = jnp.zeros((BLOCK, 2 * model_cols), jnp.float32)
        else:
            spread = jnp.repeat(carried, 2, axis=0) * ROOT_HALF
            lower_half = spread[:BLOCK]
            upper_half = spread[BLOCK:]
            upper = upper_member(position, bit_number)
            kept = jnp.where(upper, upper_half, lower_half)
            outgoing = outgoing + jnp.where(upper, lower_half, upper_half)
        carried = kept + swapped(outgoing, "ctx", bit_number)
    grads[local_levels] = grads[local_levels] + carried
    for level_index in range(all_levels - 1, 0, -1):
        grads[level_index - 1] = (
            grads[level_index - 1] + jnp.repeat(grads[level_index], 2, axis=0) * ROOT_HALF
        )
    key_grad = grads[0][:, :model_cols].astype(jnp.bfloat16)
    value_grad = grads[0][:, model_cols:].astype(jnp.bfloat16)
    return (attended, query_grad.astype(jnp.bfloat16), key_grad, value_grad)


def chunk_slot(level, head, member):
    return 2 * ((1 << level) - 2) + head * (1 << level) + member


def contract(left, right, left_dim, right_dim):
    return lax.dot_general(
        left, right, (((left_dim,), (right_dim,)), ((), ())), preferred_element_type=jnp.float32
    )


def exchange_kernel(
    levels,
    q_hbm,
    k_hbm,
    v_hbm,
    d_hbm,
    att_ref,
    dq_ref,
    dk_ref,
    dv_ref,
    k_ref,
    v_ref,
    q_ref,
    d_ref,
    wide,
    pairs,
    queried,
    pooled,
    queries_all,
    kv_all,
    grad_out,
    grad_in,
    near_out,
    near_in,
    result_out,
    result_in,
    spread,
    load_sem,
    pool_send,
    pool_recv,
    near_send,
    near_recv,
    grad_send,
    grad_recv,
    back_send,
    back_recv,
):
    me = lax.axis_index("ctx")
    count = 1 << levels
    core = lax.rem(me, 2)
    sibling = me + 1 - 2 * core
    half = 2 * HEAD_DIM
    own_cols = pl.ds(pl.multiple_of(core * half, half), half)
    sib_cols = pl.ds(pl.multiple_of(half - core * half, half), half)

    def remote(src, dst, send, recv, target):
        return pltpu.make_async_remote_copy(
            src_ref=src,
            dst_ref=dst,
            send_sem=send,
            recv_sem=recv,
            device_id={"ctx": target},
            device_id_type=pl.DeviceIdType.MESH,
        )

    barrier = pltpu.get_barrier_semaphore()
    for step in range(1, count):
        other = lax.rem(me + step, count)
        pl.semaphore_signal(
            barrier, inc=1, device_id={"ctx": other}, device_id_type=pl.DeviceIdType.MESH
        )

    loads = [
        pltpu.make_async_copy(src, dst, load_sem.at[i])
        for i, (src, dst) in enumerate(
            [(k_hbm, k_ref), (v_hbm, v_ref), (q_hbm, q_ref), (d_hbm, d_ref)]
        )
    ]
    for load in loads:
        load.start()
    for load in loads[:2]:
        load.wait()

    for c in range(2):
        for part in range(4):
            src = v_ref if part % 2 else k_ref
            low_col = c * half + part // 2 * HEAD_DIM
            column = src[:, low_col : low_col + HEAD_DIM]
            pairs[c, part // 2, :, part % 2 * HEAD_DIM : (part % 2 + 1) * HEAD_DIM] = column
            wide[c * 4 + part] = column.astype(jnp.float32)
    for level in range(1, levels):
        rows = BLOCK >> level
        base = BLOCK - 2 * rows
        for c in range(2):
            for part in range(4):
                column = wide.at[c * 4 + part]
                even = column[pl.ds(0, rows, stride=2), :]
                odd = column[pl.ds(1, rows, stride=2), :]
                low = ((even + odd) * ROOT_HALF).astype(jnp.bfloat16)
                low_col = part % 2 * HEAD_DIM
                pooled[c, part // 2, base : base + rows, low_col : low_col + HEAD_DIM] = low
                if level + 1 < levels:
                    column[0:rows, :] = low.astype(jnp.float32)
    for load in loads[2:]:
        load.wait()
    for c in range(2):
        queried[c, :, :half] = q_ref[:, c * half : (c + 1) * half]
        queried[c, :, half:] = d_ref[:, c * half : (c + 1) * half]
    pl.semaphore_wait(barrier, count - 1)

    def pool_copy(level, head, member):
        rows = BLOCK >> level
        base = BLOCK - 2 * rows
        size = 1 << level
        mine = lax.rem(me, size)
        group = lax.div(me, size)
        partner = group + 1 - 2 * lax.rem(group, 2)
        return remote(
            pooled.at[member % 2, head, pl.ds(base, rows), :],
            kv_all.at[head, pl.ds(pl.multiple_of(BLOCK * (level + 1) + mine * rows, rows), rows), :],
            pool_send.at[chunk_slot(level, head, member)],
            pool_recv.at[chunk_slot(level, head, 0) + mine],
            partner * size + member,
        )

    def pool_arrival(level, head, member):
        rows = BLOCK >> level
        base = BLOCK - 2 * rows
        return remote(
            pooled.at[0, head, pl.ds(base, rows), :],
            kv_all.at[head, pl.ds(BLOCK * (level + 1) + member * rows, rows), :],
            pool_send.at[chunk_slot(level, head, member)],
            pool_recv.at[chunk_slot(level, head, member)],
            sibling,
        )

    own_rows = pl.ds(pl.multiple_of(core * BLOCK, BLOCK), BLOCK)
    sib_rows = pl.ds(pl.multiple_of(BLOCK - core * BLOCK, BLOCK), BLOCK)
    near_pairs = [
        (queried.at[1 - core], queries_all.at[own_rows, :]),
        (pairs.at[1 - core], kv_all.at[:, own_rows, :]),
    ]
    near = [
        remote(src, dst, near_send.at[i], near_recv.at[i], sibling)
        for i, (src, dst) in enumerate(near_pairs)
    ]
    pool_copies = [
        pool_copy(level, head, member)
        for head in range(2)
        for level in reversed(range(1, levels))
        for member in range(1 << level)
    ]
    for copy in near:
        copy.start()
    for copy in pool_copies:
        copy.start()
    queries_all[own_rows, :] = queried[core]
    for h in range(2):
        kv_all[h, own_rows, :] = pairs[core, h]
    for copy in near:
        copy.wait_recv()

    segments = [(0, 2 * BLOCK)] + [(BLOCK * (level + 1), BLOCK) for level in range(1, levels)]
    score_scale = HEAD_DIM ** (-0.5)
    scores = [[], []]
    dprobs = [[], []]
    q_heads = [queries_all[:, h * HEAD_DIM : (h + 1) * HEAD_DIM] for h in range(2)]
    d_heads = [queries_all[:, half + h * HEAD_DIM : half + (h + 1) * HEAD_DIM] for h in range(2)]

    def k_part(index, h):
        low, rows = segments[index]
        return kv_all[h, low : low + rows, :HEAD_DIM]

    def v_part(index, h):
        low, rows = segments[index]
        return kv_all[h, low : low + rows, HEAD_DIM:]

    def products(index, h):
        scores[h].append(contract(q_heads[h], k_part(index, h), 1, 1) * score_scale)
        dprobs[h].append(contract(d_heads[h], v_part(index, h), 1, 1))

    for h in range(2):
        products(0, h)

    def grad_copy(level, head, member):
        rows = BLOCK >> level
        size = 1 << level
        mine = lax.rem(me, size)
        group = lax.div(me, size)
        partner = group + 1 - 2 * lax.rem(group, 2)
        return remote(
            grad_out.at[level - 1, head, pl.ds(member * rows, rows), :],
            grad_in.at[level - 1, head, pl.ds(pl.multiple_of(mine * rows, rows), rows), :],
            grad_send.at[chunk_slot(level, head, member)],
            grad_recv.at[chunk_slot(level, head, 0) + mine],
            partner * size + member,
        )

    def grad_arrival(level, head, member):
        rows = BLOCK >> level
        return remote(
            grad_out.at[level - 1, head, pl.ds(member * rows, rows), :],
            grad_in.at[level - 1, head, pl.ds(member * rows, rows), :],
            grad_send.at[chunk_slot(level, head, member)],
            grad_recv.at[chunk_slot(level, head, member)],
            sibling,
        )

    grad_copies = []
    for h in range(2):
        low_col = h * HEAD_DIM
        for index in range(1, levels):
            for member in range(1 << index):
                pool_arrival(index, h, member).wait_recv()
            products(index, h)
        peak = jnp.max(scores[h][0], axis=1, keepdims=True)
        for part in scores[h][1:]:
            peak = jnp.maximum(peak, jnp.max(part, axis=1, keepdims=True))
        weights = [jnp.exp(part - peak) for part in scores[h]]
        total = jnp.sum(weights[0], axis=1, keepdims=True)
        for part in weights[1:]:
            total = total + jnp.sum(part, axis=1, keepdims=True)
        inverse = 1.0 / total
        probs = [part * inverse for part in weights]
        probs_low = [part.astype(jnp.bfloat16) for part in probs]
        output = contract(probs_low[0], v_part(0, h), 1, 0)
        for index in range(1, levels):
            output = output + contract(probs_low[index], v_part(index, h), 1, 0)
        attended = output.astype(jnp.bfloat16)
        result_out[:, low_col : low_col + HEAD_DIM] = attended
        delta = jnp.sum(
            d_heads[h].astype(jnp.float32) * attended.astype(jnp.float32), axis=1, keepdims=True
        )
        dscores = [
            (score_scale * part * (dpart - delta)).astype(jnp.bfloat16)
            for part, dpart in zip(probs, dprobs[h])
        ]
        for index in reversed(range(1, levels)):
            grad_out[index - 1, h, :, :HEAD_DIM] = contract(
                dscores[index], q_heads[h], 0, 0
            ).astype(jnp.bfloat16)
            grad_out[index - 1, h, :, HEAD_DIM:] = contract(
                probs_low[index], d_heads[h], 0, 0
            ).astype(jnp.bfloat16)
            for member in range(1 << index):
                copy = grad_copy(index, h, member)
                copy.start()
                grad_copies.append(copy)
        near_out[h, :, :HEAD_DIM] = contract(dscores[0], q_heads[h], 0, 0).astype(jnp.bfloat16)
        near_out[h, :, HEAD_DIM:] = contract(
            probs_low[0], d_heads[h], 0, 0
        ).astype(jnp.bfloat16)
        query_total = contract(dscores[0], k_part(0, h), 1, 0)
        for index in range(1, levels):
            query_total = query_total + contract(dscores[index], k_part(index, h), 1, 0)
        result_out[:, half + low_col : half + low_col + HEAD_DIM] = query_total.astype(jnp.bfloat16)
    back = [
        remote(near_out.at[:, sib_rows, :], near_in.at[core], back_send.at[0], back_recv.at[0], sibling),
        remote(result_out.at[sib_rows, :], result_in, back_send.at[1], back_recv.at[1], sibling),
    ]
    for copy in back:
        copy.start()
    for h in range(2):
        near_in[core, h] = near_out[h, own_rows, :]
    att_ref[:, own_cols] = result_out[own_rows, :half]
    dq_ref[:, own_cols] = result_out[own_rows, half:]
    back[0].wait_recv()
    for h in range(2):
        carried = [None, None]
        for level in reversed(range(1, levels)):
            rows = BLOCK >> level
            for member in range(1 << level):
                grad_arrival(level, h, member).wait_recv()
            for c in range(2):
                for member in range(c, 1 << level, 2):
                    part = grad_in[level - 1, h, member * rows : (member + 1) * rows, :].astype(jnp.float32)
                    carried[c] = part if carried[c] is None else carried[c] + part
                carried[c] = carried[c] * ROOT_HALF
                for place in range(2):
                    column = spread.at[2 * c + place]
                    piece = carried[c][:, place * HEAD_DIM : (place + 1) * HEAD_DIM]
                    column[pl.ds(0, rows, stride=2), :] = piece
                    column[pl.ds(1, rows, stride=2), :] = piece
                carried[c] = jnp.concatenate(
                    [spread[2 * c + place, 0 : 2 * rows, :] for place in range(2)], axis=1
                )
        for c in range(2):
            low = (carried[c] + near_in[c, h].astype(jnp.float32)).astype(jnp.bfloat16)
            low_col = c * half + h * HEAD_DIM
            dk_ref[:, low_col : low_col + HEAD_DIM] = low[:, :HEAD_DIM]
            dv_ref[:, low_col : low_col + HEAD_DIM] = low[:, HEAD_DIM:]
    back[1].wait_recv()
    att_ref[:, sib_cols] = result_in[:, :half]
    dq_ref[:, sib_cols] = result_in[:, half:]
    for copy in near + pool_copies + grad_copies + back:
        copy.wait_send()


def place_kernel(*refs):
    sources, results, held, arrive, leave = refs[:4], refs[4:8], refs[8], refs[9], refs[10]
    inward = [pltpu.make_async_copy(sources[i], held.at[i], arrive.at[i]) for i in range(4)]
    outward = [pltpu.make_async_copy(held.at[i], results[i], leave.at[i]) for i in range(4)]
    for copy in inward:
        copy.start()
    for first, second in zip(inward, outward):
        first.wait()
        second.start()
    for copy in outward:
        copy.wait()


def per_device(queries, keys, values, cotangent):
    tok_count, model_cols = queries.shape
    levels = lax.axis_size("ctx").bit_length() - 1
    if tok_count != BLOCK or levels < 2 or BLOCK >> (levels - 1) < 16:
        return per_device_chained(queries, keys, values, cotangent)
    chunks = 2 * ((1 << levels) - 2)
    half = model_cols // 2
    flat = jax.ShapeDtypeStruct((tok_count, model_cols), jnp.bfloat16)
    vmem = pl.BlockSpec(memory_space=pltpu.VMEM)
    results = pl.pallas_call(
        functools.partial(exchange_kernel, levels),
        out_shape=(flat, flat, flat, flat),
        in_specs=[pl.BlockSpec(memory_space=pl.ANY)] * 4,
        out_specs=(vmem,) * 4,
        scratch_shapes=[
            pltpu.VMEM((BLOCK, model_cols), jnp.bfloat16),
            pltpu.VMEM((BLOCK, model_cols), jnp.bfloat16),
            pltpu.VMEM((BLOCK, model_cols), jnp.bfloat16),
            pltpu.VMEM((BLOCK, model_cols), jnp.bfloat16),
            pltpu.VMEM((8, BLOCK, HEAD_DIM), jnp.float32),
            pltpu.VMEM((2, 2, BLOCK, half), jnp.bfloat16),
            pltpu.VMEM((2, BLOCK, model_cols), jnp.bfloat16),
            pltpu.VMEM((2, 2, BLOCK, half), jnp.bfloat16),
            pltpu.VMEM((2 * BLOCK, model_cols), jnp.bfloat16),
            pltpu.VMEM((2, BLOCK * (levels + 1), half), jnp.bfloat16),
            pltpu.VMEM((levels - 1, 2, BLOCK, half), jnp.bfloat16),
            pltpu.VMEM((levels - 1, 2, BLOCK, half), jnp.bfloat16),
            pltpu.VMEM((2, 2 * BLOCK, half), jnp.bfloat16),
            pltpu.VMEM((2, 2, BLOCK, half), jnp.bfloat16),
            pltpu.VMEM((2 * BLOCK, model_cols), jnp.bfloat16),
            pltpu.VMEM((BLOCK, model_cols), jnp.bfloat16),
            pltpu.VMEM((4, BLOCK, HEAD_DIM), jnp.float32),
            pltpu.SemaphoreType.DMA((4,)),
            pltpu.SemaphoreType.DMA((chunks,)),
            pltpu.SemaphoreType.DMA((chunks,)),
            pltpu.SemaphoreType.DMA((2,)),
            pltpu.SemaphoreType.DMA((2,)),
            pltpu.SemaphoreType.DMA((chunks,)),
            pltpu.SemaphoreType.DMA((chunks,)),
            pltpu.SemaphoreType.DMA((2,)),
            pltpu.SemaphoreType.DMA((2,)),
        ],
        compiler_params=pltpu.CompilerParams(
            collective_id=0, has_side_effects=True, vmem_limit_bytes=56 * 1024 * 1024
        ),
    )(queries, keys, values, cotangent)
    anywhere = pl.BlockSpec(memory_space=pl.ANY)
    return pl.pallas_call(
        place_kernel,
        out_shape=(flat, flat, flat, flat),
        in_specs=[anywhere] * 4,
        out_specs=(anywhere,) * 4,
        scratch_shapes=[
            pltpu.VMEM((4, tok_count, model_cols), jnp.bfloat16),
            pltpu.SemaphoreType.DMA((4,)),
            pltpu.SemaphoreType.DMA((4,)),
        ],
        compiler_params=pltpu.CompilerParams(vmem_limit_bytes=56 * 1024 * 1024),
    )(*results)


def solution(mesh):
    placed = (
        P(("groups", "ctx"), None),
        P(("groups", "ctx"), None),
        P(("groups", "ctx"), None),
        P(("groups", "ctx"), None),
    )
    return jax.shard_map(
        per_device,
        mesh=mesh,
        in_specs=placed,
        out_specs=(
            P(("groups", "ctx"), None),
            P(("groups", "ctx"), None),
            P(("groups", "ctx"), None),
            P(("groups", "ctx"), None),
        ),
        check_vma=False,
    )
```

```python
import functools

import jax
import jax.numpy as jnp
from jax import lax
from jax.experimental import pallas as pl
from jax.experimental.pallas import tpu as pltpu
from jax.sharding import PartitionSpec as P

HEADS = 4
HEAD_DIM = 128
BLOCK = 128


ROOT_HALF = 0.70710678


def swapped(value, axis, stride):
    mask = 2**stride
    pairs = [(source, source ^ mask) for source in range(lax.axis_size(axis))]
    return lax.ppermute(value, axis, pairs)


def pool_rows(pairs):
    widened = pairs.astype(jnp.float32).reshape(pairs.shape[0] // 2, 2, pairs.shape[1])
    return ((widened[:, 0] + widened[:, 1]) * ROOT_HALF).astype(jnp.bfloat16)


def attend_sets(queries, cotangent, pair_sets, groups):
    row_count = queries.shape[0]
    model_cols = queries.shape[1]
    set_width = pair_sets[0].shape[1]
    score_scale = HEAD_DIM ** (-0.5)
    attended_heads = []
    query_heads = []
    key_heads = [[] for member in pair_sets]
    value_heads = [[] for member in pair_sets]
    for head_index in range(HEADS):
        low_col = head_index * HEAD_DIM
        q_head = queries[:, low_col : low_col + HEAD_DIM]
        d_head = cotangent[:, low_col : low_col + HEAD_DIM]
        key_parts = []
        value_parts = []
        score_list = []
        for pair_set, group_size in zip(pair_sets, groups):
            key_part = pair_set[:, :, low_col : low_col + HEAD_DIM]
            value_part = pair_set[:, :, model_cols + low_col : model_cols + low_col + HEAD_DIM]
            key_parts.append(key_part)
            value_parts.append(value_part)
            q_group = q_head.reshape(row_count // group_size, group_size, HEAD_DIM)
            score_list.append(
                jnp.einsum(
                    "gsd,gkd->gsk", q_group, key_part, preferred_element_type=jnp.float32
                ).reshape(row_count, set_width)
            )
        scores = jnp.stack(score_list, axis=0) * score_scale
        peak = jnp.max(scores, axis=(0, 2))
        weights = jnp.exp(scores - peak[None, :, None])
        probs = weights / jnp.sum(weights, axis=(0, 2))[None, :, None]
        probs_low = probs.astype(jnp.bfloat16)
        output = jnp.zeros((row_count, HEAD_DIM), jnp.float32)
        dprob_list = []
        for set_index in range(len(pair_sets)):
            group_size = groups[set_index]
            p_group = probs_low[set_index].reshape(row_count // group_size, group_size, set_width)
            output = output + jnp.einsum(
                "gsk,gkd->gsd", p_group, value_parts[set_index], preferred_element_type=jnp.float32
            ).reshape(row_count, HEAD_DIM)
            d_group = d_head.reshape(row_count // group_size, group_size, HEAD_DIM)
            dprob_list.append(
                jnp.einsum(
                    "gsd,gkd->gsk",
                    d_group,
                    value_parts[set_index],
                    preferred_element_type=jnp.float32,
                ).reshape(row_count, set_width)
            )
        attended = output.astype(jnp.bfloat16)
        delta = jnp.sum(d_head.astype(jnp.float32) * attended.astype(jnp.float32), axis=1)
        dprobs = jnp.stack(dprob_list, axis=0)
        dscores = (score_scale * probs * (dprobs - delta[None, :, None])).astype(jnp.bfloat16)
        query_total = jnp.zeros((row_count, HEAD_DIM), jnp.float32)
        for set_index in range(len(pair_sets)):
            group_size = groups[set_index]
            s_group = dscores[set_index].reshape(row_count // group_size, group_size, set_width)
            p_group = probs_low[set_index].reshape(row_count // group_size, group_size, set_width)
            q_group = q_head.reshape(row_count // group_size, group_size, HEAD_DIM)
            d_group = d_head.reshape(row_count // group_size, group_size, HEAD_DIM)
            query_total = query_total + jnp.einsum(
                "gsk,gkd->gsd", s_group, key_parts[set_index], preferred_element_type=jnp.float32
            ).reshape(row_count, HEAD_DIM)
            key_heads[set_index].append(
                jnp.einsum("gsk,gsd->gkd", s_group, q_group, preferred_element_type=jnp.float32)
            )
            value_heads[set_index].append(
                jnp.einsum("gsk,gsd->gkd", p_group, d_group, preferred_element_type=jnp.float32)
            )
        attended_heads.append(attended)
        query_heads.append(query_total)
    set_grads = [
        jnp.concatenate(key_heads[set_index] + value_heads[set_index], axis=2)
        for set_index in range(len(pair_sets))
    ]
    return (
        jnp.concatenate(attended_heads, axis=1),
        jnp.concatenate(query_heads, axis=1),
        set_grads,
    )


def upper_member(position, bit_number):
    return position // (1 << bit_number) % 2 == 1


def per_device_chained(queries, keys, values, cotangent):
    tok_count, model_cols = queries.shape
    ctx_count = lax.axis_size("ctx")
    position = lax.axis_index("ctx")
    block_count = tok_count // BLOCK
    local_levels = block_count.bit_length() - 1
    all_levels = (block_count * ctx_count).bit_length() - 1
    pair_level = [jnp.concatenate([keys, values], axis=1)]
    for level_index in range(1, all_levels):
        pair_level.append(pool_rows(pair_level[-1]))
    pair_sets = [pair_level[0].reshape(block_count, BLOCK, 2 * model_cols)]
    groups = [BLOCK]
    far_pairs = [None for level_index in range(local_levels, all_levels)]
    own_pairs = pair_level[local_levels]
    for level_index in range(local_levels, all_levels):
        bit_number = level_index - local_levels
        received = swapped(own_pairs, "ctx", bit_number)
        far_pairs[bit_number] = received
        if level_index + 1 < all_levels:
            upper = upper_member(position, bit_number)
            joined = jnp.where(
                upper,
                jnp.concatenate([received, own_pairs], axis=0),
                jnp.concatenate([own_pairs, received], axis=0),
            )
            own_pairs = pool_rows(joined)
    for level_index in range(local_levels, all_levels):
        pair_sets.append(far_pairs[level_index - local_levels].reshape(1, BLOCK, 2 * model_cols))
        groups.append(tok_count)
    attended, query_grad, set_grads = attend_sets(queries, cotangent, pair_sets, groups)
    grads = [
        jnp.zeros((tok_count >> level_index, 2 * model_cols), jnp.float32)
        for level_index in range(all_levels)
    ]
    grads[0] = set_grads[0].reshape(tok_count, 2 * model_cols)
    far_grads = [
        set_grads[1 + level_index].reshape(BLOCK, 2 * model_cols)
        for level_index in range(local_levels, all_levels)
    ]
    carried = None
    for level_index in reversed(range(local_levels, all_levels)):
        bit_number = level_index - local_levels
        outgoing = far_grads[bit_number]
        if carried is None:
            kept = jnp.zeros((BLOCK, 2 * model_cols), jnp.float32)
        else:
            spread = jnp.repeat(carried, 2, axis=0) * ROOT_HALF
            lower_half = spread[:BLOCK]
            upper_half = spread[BLOCK:]
            upper = upper_member(position, bit_number)
            kept = jnp.where(upper, upper_half, lower_half)
            outgoing = outgoing + jnp.where(upper, lower_half, upper_half)
        carried = kept + swapped(outgoing, "ctx", bit_number)
    grads[local_levels] = grads[local_levels] + carried
    for level_index in range(all_levels - 1, 0, -1):
        grads[level_index - 1] = (
            grads[level_index - 1] + jnp.repeat(grads[level_index], 2, axis=0) * ROOT_HALF
        )
    key_grad = grads[0][:, :model_cols].astype(jnp.bfloat16)
    value_grad = grads[0][:, model_cols:].astype(jnp.bfloat16)
    return (attended, query_grad.astype(jnp.bfloat16), key_grad, value_grad)


def chunk_slot(level, head, member):
    return 2 * ((1 << level) - 2) + head * (1 << level) + member


def contract(left, right, left_dim, right_dim):
    return lax.dot_general(
        left, right, (((left_dim,), (right_dim,)), ((), ())), preferred_element_type=jnp.float32
    )


def exchange_kernel(
    levels,
    q_hbm,
    k_hbm,
    v_hbm,
    d_hbm,
    att_hbm,
    dq_hbm,
    dk_hbm,
    dv_hbm,
    att_ref,
    dq_ref,
    dk_ref,
    dv_ref,
    k_ref,
    v_ref,
    q_ref,
    d_ref,
    wide,
    pairs,
    queried,
    pooled,
    queries_all,
    kv_all,
    grad_out,
    grad_in,
    near_out,
    near_in,
    result_out,
    result_in,
    spread,
    load_sem,
    store_sem,
    pool_send,
    pool_recv,
    near_send,
    near_recv,
    grad_send,
    grad_recv,
    back_send,
    back_recv,
):
    me = lax.axis_index("ctx")
    count = 1 << levels
    core = lax.rem(me, 2)
    sibling = me + 1 - 2 * core
    half = 2 * HEAD_DIM
    own_cols = pl.ds(pl.multiple_of(core * half, half), half)
    sib_cols = pl.ds(pl.multiple_of(half - core * half, half), half)

    def remote(src, dst, send, recv, target):
        return pltpu.make_async_remote_copy(
            src_ref=src,
            dst_ref=dst,
            send_sem=send,
            recv_sem=recv,
            device_id={"ctx": target},
            device_id_type=pl.DeviceIdType.MESH,
        )

    barrier = pltpu.get_barrier_semaphore()
    for step in range(1, count):
        other = lax.rem(me + step, count)
        pl.semaphore_signal(
            barrier, inc=1, device_id={"ctx": other}, device_id_type=pl.DeviceIdType.MESH
        )

    loads = [
        pltpu.make_async_copy(src, dst, load_sem.at[i])
        for i, (src, dst) in enumerate(
            [(k_hbm, k_ref), (v_hbm, v_ref), (q_hbm, q_ref), (d_hbm, d_ref)]
        )
    ]
    for load in loads:
        load.start()
    for load in loads[:2]:
        load.wait()

    for c in range(2):
        for part in range(4):
            src = v_ref if part % 2 else k_ref
            low_col = c * half + part // 2 * HEAD_DIM
            column = src[:, low_col : low_col + HEAD_DIM]
            pairs[c, part // 2, :, part % 2 * HEAD_DIM : (part % 2 + 1) * HEAD_DIM] = column
            wide[c * 4 + part] = column.astype(jnp.float32)
    for level in range(1, levels):
        rows = BLOCK >> level
        base = BLOCK - 2 * rows
        for c in range(2):
            for part in range(4):
                column = wide.at[c * 4 + part]
                even = column[pl.ds(0, rows, stride=2), :]
                odd = column[pl.ds(1, rows, stride=2), :]
                low = ((even + odd) * ROOT_HALF).astype(jnp.bfloat16)
                low_col = part % 2 * HEAD_DIM
                pooled[c, part // 2, base : base + rows, low_col : low_col + HEAD_DIM] = low
                if level + 1 < levels:
                    column[0:rows, :] = low.astype(jnp.float32)
    for load in loads[2:]:
        load.wait()
    for c in range(2):
        queried[c, :, :half] = q_ref[:, c * half : (c + 1) * half]
        queried[c, :, half:] = d_ref[:, c * half : (c + 1) * half]
    pl.semaphore_wait(barrier, count - 1)

    def pool_copy(level, head, member):
        rows = BLOCK >> level
        base = BLOCK - 2 * rows
        size = 1 << level
        mine = lax.rem(me, size)
        group = lax.div(me, size)
        partner = group + 1 - 2 * lax.rem(group, 2)
        return remote(
            pooled.at[member % 2, head, pl.ds(base, rows), :],
            kv_all.at[head, pl.ds(pl.multiple_of(BLOCK * (level + 1) + mine * rows, rows), rows), :],
            pool_send.at[chunk_slot(level, head, member)],
            pool_recv.at[chunk_slot(level, head, 0) + mine],
            partner * size + member,
        )

    def pool_arrival(level, head, member):
        rows = BLOCK >> level
        base = BLOCK - 2 * rows
        return remote(
            pooled.at[0, head, pl.ds(base, rows), :],
            kv_all.at[head, pl.ds(BLOCK * (level + 1) + member * rows, rows), :],
            pool_send.at[chunk_slot(level, head, member)],
            pool_recv.at[chunk_slot(level, head, member)],
            sibling,
        )

    own_rows = pl.ds(pl.multiple_of(core * BLOCK, BLOCK), BLOCK)
    sib_rows = pl.ds(pl.multiple_of(BLOCK - core * BLOCK, BLOCK), BLOCK)
    near_pairs = [
        (queried.at[1 - core], queries_all.at[own_rows, :]),
        (pairs.at[1 - core, 0], kv_all.at[0, own_rows, :]),
        (pairs.at[1 - core, 1], kv_all.at[1, own_rows, :]),
    ]
    near = [
        remote(src, dst, near_send.at[i], near_recv.at[i], sibling)
        for i, (src, dst) in enumerate(near_pairs)
    ]
    pool_copies = [
        pool_copy(level, head, member)
        for head in range(2)
        for level in reversed(range(1, levels))
        for member in range(1 << level)
    ]
    for copy in near:
        copy.start()
    for copy in pool_copies:
        copy.start()
    queries_all[own_rows, :] = queried[core]
    for h in range(2):
        kv_all[h, own_rows, :] = pairs[core, h]
    for copy in near:
        copy.wait_recv()

    segments = [(0, 2 * BLOCK)] + [(BLOCK * (level + 1), BLOCK) for level in range(1, levels)]
    score_scale = HEAD_DIM ** (-0.5)
    scores = [[], []]
    dprobs = [[], []]
    q_heads = [queries_all[:, h * HEAD_DIM : (h + 1) * HEAD_DIM] for h in range(2)]
    d_heads = [queries_all[:, half + h * HEAD_DIM : half + (h + 1) * HEAD_DIM] for h in range(2)]

    def k_part(index, h):
        low, rows = segments[index]
        return kv_all[h, low : low + rows, :HEAD_DIM]

    def v_part(index, h):
        low, rows = segments[index]
        return kv_all[h, low : low + rows, HEAD_DIM:]

    def products(index, h):
        scores[h].append(contract(q_heads[h], k_part(index, h), 1, 1) * score_scale)
        dprobs[h].append(contract(d_heads[h], v_part(index, h), 1, 1))

    for h in range(2):
        products(0, h)

    def grad_copy(level, head, member):
        rows = BLOCK >> level
        size = 1 << level
        mine = lax.rem(me, size)
        group = lax.div(me, size)
        partner = group + 1 - 2 * lax.rem(group, 2)
        return remote(
            grad_out.at[level - 1, head, pl.ds(member * rows, rows), :],
            grad_in.at[level - 1, head, pl.ds(pl.multiple_of(mine * rows, rows), rows), :],
            grad_send.at[chunk_slot(level, head, member)],
            grad_recv.at[chunk_slot(level, head, 0) + mine],
            partner * size + member,
        )

    def grad_arrival(level, head, member):
        rows = BLOCK >> level
        return remote(
            grad_out.at[level - 1, head, pl.ds(member * rows, rows), :],
            grad_in.at[level - 1, head, pl.ds(member * rows, rows), :],
            grad_send.at[chunk_slot(level, head, member)],
            grad_recv.at[chunk_slot(level, head, member)],
            sibling,
        )

    grad_copies = []
    for h in range(2):
        low_col = h * HEAD_DIM
        for index in range(1, levels):
            for member in range(1 << index):
                pool_arrival(index, h, member).wait_recv()
            products(index, h)
        peak = jnp.max(scores[h][0], axis=1, keepdims=True)
        for part in scores[h][1:]:
            peak = jnp.maximum(peak, jnp.max(part, axis=1, keepdims=True))
        weights = [jnp.exp(part - peak) for part in scores[h]]
        total = jnp.sum(weights[0], axis=1, keepdims=True)
        for part in weights[1:]:
            total = total + jnp.sum(part, axis=1, keepdims=True)
        inverse = 1.0 / total
        probs = [part * inverse for part in weights]
        probs_low = [part.astype(jnp.bfloat16) for part in probs]
        output = contract(probs_low[0], v_part(0, h), 1, 0)
        for index in range(1, levels):
            output = output + contract(probs_low[index], v_part(index, h), 1, 0)
        attended = output.astype(jnp.bfloat16)
        result_out[:, low_col : low_col + HEAD_DIM] = attended
        delta = jnp.sum(
            d_heads[h].astype(jnp.float32) * attended.astype(jnp.float32), axis=1, keepdims=True
        )
        dscores = [
            (score_scale * part * (dpart - delta)).astype(jnp.bfloat16)
            for part, dpart in zip(probs, dprobs[h])
        ]
        for index in reversed(range(1, levels)):
            grad_out[index - 1, h, :, :HEAD_DIM] = contract(
                dscores[index], q_heads[h], 0, 0
            ).astype(jnp.bfloat16)
            grad_out[index - 1, h, :, HEAD_DIM:] = contract(
                probs_low[index], d_heads[h], 0, 0
            ).astype(jnp.bfloat16)
            for member in range(1 << index):
                copy = grad_copy(index, h, member)
                copy.start()
                grad_copies.append(copy)
        near_out[h, :, :HEAD_DIM] = contract(dscores[0], q_heads[h], 0, 0).astype(jnp.bfloat16)
        near_out[h, :, HEAD_DIM:] = contract(
            probs_low[0], d_heads[h], 0, 0
        ).astype(jnp.bfloat16)
        query_total = contract(dscores[0], k_part(0, h), 1, 0)
        for index in range(1, levels):
            query_total = query_total + contract(dscores[index], k_part(index, h), 1, 0)
        result_out[:, half + low_col : half + low_col + HEAD_DIM] = query_total.astype(jnp.bfloat16)
    back = [
        remote(near_out.at[h, sib_rows, :], near_in.at[core, h], back_send.at[h], back_recv.at[h], sibling)
        for h in range(2)
    ] + [
        remote(result_out.at[sib_rows, :], result_in, back_send.at[2], back_recv.at[2], sibling),
    ]
    for copy in back:
        copy.start()
    for h in range(2):
        near_in[core, h] = near_out[h, own_rows, :]
    att_ref[:, own_cols] = result_out[own_rows, :half]
    dq_ref[:, own_cols] = result_out[own_rows, half:]
    back[2].wait_recv()
    att_ref[:, sib_cols] = result_in[:, :half]
    dq_ref[:, sib_cols] = result_in[:, half:]
    stores = [
        pltpu.make_async_copy(src, dst, store_sem.at[i])
        for i, (src, dst) in enumerate(
            [(att_ref, att_hbm), (dq_ref, dq_hbm), (dk_ref, dk_hbm), (dv_ref, dv_hbm)]
        )
    ]
    for store in stores[:2]:
        store.start()
    for copy in back[:2]:
        copy.wait_recv()
    for h in range(2):
        carried = [None, None]
        for level in reversed(range(1, levels)):
            rows = BLOCK >> level
            for member in range(1 << level):
                grad_arrival(level, h, member).wait_recv()
            for c in range(2):
                for member in range(c, 1 << level, 2):
                    part = grad_in[level - 1, h, member * rows : (member + 1) * rows, :].astype(jnp.float32)
                    carried[c] = part if carried[c] is None else carried[c] + part
                carried[c] = carried[c] * ROOT_HALF
                for place in range(2):
                    column = spread.at[2 * c + place]
                    piece = carried[c][:, place * HEAD_DIM : (place + 1) * HEAD_DIM]
                    column[pl.ds(0, rows, stride=2), :] = piece
                    column[pl.ds(1, rows, stride=2), :] = piece
                carried[c] = jnp.concatenate(
                    [spread[2 * c + place, 0 : 2 * rows, :] for place in range(2)], axis=1
                )
        for c in range(2):
            low = (carried[c] + near_in[c, h].astype(jnp.float32)).astype(jnp.bfloat16)
            low_col = c * half + h * HEAD_DIM
            dk_ref[:, low_col : low_col + HEAD_DIM] = low[:, :HEAD_DIM]
            dv_ref[:, low_col : low_col + HEAD_DIM] = low[:, HEAD_DIM:]
    for store in stores[2:]:
        store.start()
    for store in stores:
        store.wait()
    for copy in near + pool_copies + grad_copies + back:
        copy.wait_send()


def place_kernel(*refs):
    sources, results, held, arrive, leave = refs[:4], refs[4:8], refs[8], refs[9], refs[10]
    inward = [pltpu.make_async_copy(sources[i], held.at[i], arrive.at[i]) for i in range(4)]
    outward = [pltpu.make_async_copy(held.at[i], results[i], leave.at[i]) for i in range(4)]
    for copy in inward:
        copy.start()
    for first, second in zip(inward, outward):
        first.wait()
        second.start()
    for copy in outward:
        copy.wait()


def per_device(queries, keys, values, cotangent):
    tok_count, model_cols = queries.shape
    levels = lax.axis_size("ctx").bit_length() - 1
    if tok_count != BLOCK or levels < 2 or BLOCK >> (levels - 1) < 16:
        return per_device_chained(queries, keys, values, cotangent)
    chunks = 2 * ((1 << levels) - 2)
    half = model_cols // 2
    flat = jax.ShapeDtypeStruct((tok_count, model_cols), jnp.bfloat16)
    anywhere = pl.BlockSpec(memory_space=pl.ANY)
    results = pl.pallas_call(
        functools.partial(exchange_kernel, levels),
        out_shape=(flat, flat, flat, flat),
        in_specs=[anywhere] * 4,
        out_specs=(anywhere,) * 4,
        scratch_shapes=[
            pltpu.VMEM((BLOCK, model_cols), jnp.bfloat16),
            pltpu.VMEM((BLOCK, model_cols), jnp.bfloat16),
            pltpu.VMEM((BLOCK, model_cols), jnp.bfloat16),
            pltpu.VMEM((BLOCK, model_cols), jnp.bfloat16),
            pltpu.VMEM((BLOCK, model_cols), jnp.bfloat16),
            pltpu.VMEM((BLOCK, model_cols), jnp.bfloat16),
            pltpu.VMEM((BLOCK, model_cols), jnp.bfloat16),
            pltpu.VMEM((BLOCK, model_cols), jnp.bfloat16),
            pltpu.VMEM((8, BLOCK, HEAD_DIM), jnp.float32),
            pltpu.VMEM((2, 2, BLOCK, half), jnp.bfloat16),
            pltpu.VMEM((2, BLOCK, model_cols), jnp.bfloat16),
            pltpu.VMEM((2, 2, BLOCK, half), jnp.bfloat16),
            pltpu.VMEM((2 * BLOCK, model_cols), jnp.bfloat16),
            pltpu.VMEM((2, BLOCK * (levels + 1), half), jnp.bfloat16),
            pltpu.VMEM((levels - 1, 2, BLOCK, half), jnp.bfloat16),
            pltpu.VMEM((levels - 1, 2, BLOCK, half), jnp.bfloat16),
            pltpu.VMEM((2, 2 * BLOCK, half), jnp.bfloat16),
            pltpu.VMEM((2, 2, BLOCK, half), jnp.bfloat16),
            pltpu.VMEM((2 * BLOCK, model_cols), jnp.bfloat16),
            pltpu.VMEM((BLOCK, model_cols), jnp.bfloat16),
            pltpu.VMEM((4, BLOCK, HEAD_DIM), jnp.float32),
            pltpu.SemaphoreType.DMA((4,)),
            pltpu.SemaphoreType.DMA((4,)),
            pltpu.SemaphoreType.DMA((chunks,)),
            pltpu.SemaphoreType.DMA((chunks,)),
            pltpu.SemaphoreType.DMA((3,)),
            pltpu.SemaphoreType.DMA((3,)),
            pltpu.SemaphoreType.DMA((chunks,)),
            pltpu.SemaphoreType.DMA((chunks,)),
            pltpu.SemaphoreType.DMA((3,)),
            pltpu.SemaphoreType.DMA((3,)),
        ],
        compiler_params=pltpu.CompilerParams(
            collective_id=0, has_side_effects=True, vmem_limit_bytes=56 * 1024 * 1024
        ),
    )(queries, keys, values, cotangent)
    return pl.pallas_call(
        place_kernel,
        out_shape=(flat, flat, flat, flat),
        in_specs=[anywhere] * 4,
        out_specs=(anywhere,) * 4,
        scratch_shapes=[
            pltpu.VMEM((4, tok_count, model_cols), jnp.bfloat16),
            pltpu.SemaphoreType.DMA((4,)),
            pltpu.SemaphoreType.DMA((4,)),
        ],
        compiler_params=pltpu.CompilerParams(vmem_limit_bytes=56 * 1024 * 1024),
    )(*results)


def solution(mesh):
    placed = (
        P(("groups", "ctx"), None),
        P(("groups", "ctx"), None),
        P(("groups", "ctx"), None),
        P(("groups", "ctx"), None),
    )
    return jax.shard_map(
        per_device,
        mesh=mesh,
        in_specs=placed,
        out_specs=(
            P(("groups", "ctx"), None),
            P(("groups", "ctx"), None),
            P(("groups", "ctx"), None),
            P(("groups", "ctx"), None),
        ),
        check_vma=False,
    )
```
